128 devices in a mesh: group: 2 (over z_lo), seq: 8 (over x, core), head: 8 (over z_hi, y).
Axes of the slice: x: 4, y: 4, z: 4 (z_hi: 2, z_lo: 2; z = z_hi * 2 + z_lo), core: 2. Of those that a mesh axis runs over, the one named last changes fastest.
Arguments:
- prompt_kv: bfloat16 [2, 32768, 1024], P(None, ('group', 'seq'), 'head'), may hold values from -16 to 16
- queries: bfloat16 [3, 256, 16384], P(None, 'group', 'head'), may hold values from -32 to 32
- new_kv: bfloat16 [2, 3, 256, 1024], P(None, None, 'group', 'head'), may hold values from -16 to 16
- resident_kv: bfloat16 [2, 256, 1024, 1024], P(None, 'group', 'seq', 'head'), may hold values from -8 to 8
- seq_lengths: int32 [256], P('group'), may hold values from 1 to 1024, 131072 in all
Outputs:
- attended: bfloat16 [3, 256, 16384], P(None, 'group', 'head')
The draws below stay inside these ranges and needn't reach their ends.
Inputs may be any that keep to these rules, and one draw needn't show every extreme that they name: `seq_lengths`: some sample has all 1024 slots valid.
All inputs are finite; a program needn't handle non-finite values. No bound on the sum of `seq_lengths` on one device may be relied on, other than what follows from the above.
Results may differ from the reference program's by a relative error of at most 0.0045.
Values may be sent and summed in bfloat16 or wider, within the bound.
A program may use at most 128 MiB of HBM per device.

```python
import math
import jax
import jax.numpy as jnp
import numpy as np
from jax import lax

QH = 128
KVH = 8
DH = 128
STEPS = 3
PROMPT = 32768
SAMPLES = 256
RES = 1024


def shared_parts(key):
    direction = jax.random.normal(jax.random.fold_in(key, 101), (STEPS, SAMPLES, KVH, DH), jnp.float32)
    return direction


def draw_prompt_kv(key, part):
    key = jax.random.fold_in(key, 3)
    key_rows = jax.random.normal(jax.random.fold_in(key, 1), (PROMPT, KVH, DH), jnp.float32)
    value_rows = jax.random.normal(jax.random.fold_in(key, 2), (PROMPT, KVH, DH), jnp.float32)
    key_rows = jnp.clip(key_rows, -16.0, 16.0)
    value_rows = jnp.clip(value_rows, -6.0, 6.0)
    return jnp.stack([key_rows, value_rows]).reshape(2, PROMPT, KVH * DH).astype(jnp.bfloat16)


def draw_queries(key, part):
    direction = shared_parts(key)
    key = jax.random.fold_in(key, 5)
    own_noise = jax.random.normal(jax.random.fold_in(key, 1), (STEPS, SAMPLES, KVH, QH // KVH, DH), jnp.float32)
    query_rows = 1.5 * (0.8 * direction[:, :, :, None, :] + 0.6 * own_noise)
    loose_signs = jnp.where(jax.random.bernoulli(jax.random.fold_in(key, 3), 0.5, (4, KVH, QH // KVH, DH)), 1.0, -1.0).astype(jnp.float32)
    query_rows = query_rows.at[1, :4].set(28.0 * loose_signs)
    query_rows = jnp.clip(query_rows, -32.0, 32.0)
    return query_rows.reshape(STEPS, SAMPLES, QH * DH).astype(jnp.bfloat16)


def draw_new_kv(key, part):
    direction = shared_parts(key)
    key = jax.random.fold_in(key, 7)
    key_rows = 0.35 * direction + 0.92 * jax.random.normal(jax.random.fold_in(key, 1), (STEPS, SAMPLES, KVH, DH), jnp.float32)
    value_rows = jax.random.normal(jax.random.fold_in(key, 2), (STEPS, SAMPLES, KVH, DH), jnp.float32)
    key_rows = jnp.clip(key_rows, -16.0, 16.0)
    value_rows = jnp.clip(value_rows, -6.0, 6.0)
    return jnp.stack([key_rows, value_rows]).reshape(2, STEPS, SAMPLES, KVH * DH).astype(jnp.bfloat16)


def block_scale(rng, dims, cuts, smallest, high):
    def one(dim, parts):
        draws = jax.random.uniform(jax.random.fold_in(jax.random.fold_in(rng, 6), dim), (parts,), jnp.float32, smallest / len(cuts), high / len(cuts))
        return jnp.repeat(jnp.exp(draws), dims[dim] // parts).reshape((-1,) + (1,) * (len(dims) - dim - 1))

    factor_of = one(*cuts[0])
    for cut in cuts[1:]:
        factor_of = factor_of * one(*cut)
    return factor_of


def split_up(amount, total, bound, lean):
    loads = [(1 << 20) // math.isqrt(standing ** lean) + 1 for standing in range(2, amount + 1)]
    spare, given = total - bound - (amount - 1), [1] * (amount - 1)
    while spare > 0:
        free = [i for i in range(amount - 1) if given[i] < bound]
        pool, budget = sum([loads[i] for i in free]), spare
        for i in free:
            addition = min(bound - given[i], max(1, budget * loads[i] // pool), spare)
            given[i] = given[i] + addition
            spare = spare - addition
    return np.array([bound] + given)


def uneven_parts(stream_key, count, total, reach, lean):
    if count == 2:
        one = jax.random.randint(stream_key, (), max(1, total - reach), min(reach, total - 1) + 1)
        return jnp.stack([one, total - one])
    tallies = jnp.asarray(split_up(count, total, reach, lean), jnp.int32)
    twos = (count - 1) // 2
    giver, receiver = tallies[1:1 + 2 * twos:2], tallies[2:2 + 2 * twos:2]
    slack = jnp.minimum(giver - 1, reach - receiver)
    passed = jax.random.randint(jax.random.fold_in(stream_key, 1), (twos,), 0, 1 << 20) % (slack + 1)
    tallies = tallies.at[1:1 + 2 * twos:2].set(giver - passed).at[2:2 + 2 * twos:2].set(receiver + passed)
    return tallies[jax.random.permutation(jax.random.fold_in(stream_key, 2), count)]


def gaussian(stream_key, extent, deviation, bound, split=(), held_as=jnp.bfloat16):
    values = deviation * jax.random.normal(stream_key, extent, jnp.float32)
    if split:
        values = values * block_scale(stream_key, extent, split, -0.22, 0.18)
    return jnp.clip(values, -bound, bound).astype(held_as)


def setup_inputs(seed: int = 0) -> dict:
    splits = jax.random.split(jax.random.key(seed), 6)
    return {
        "prompt_kv": draw_prompt_kv(jax.random.fold_in(splits[5], 71), 0),
        "queries": draw_queries(jax.random.fold_in(splits[5], 71), 0),
        "new_kv": draw_new_kv(jax.random.fold_in(splits[5], 71), 0),
        "resident_kv": gaussian(splits[3], (2, SAMPLES, RES, KVH * DH), 1.3, 8.0, ((1, 2), (2, 8), (3, 8))),
        "seq_lengths": uneven_parts(splits[4], SAMPLES, SAMPLES * RES // 2, RES, 2).astype(jnp.int32),
    }


MASKED_SCORE = -1e30


def lowered_precision_weights(weights):
    return lax.optimization_barrier(weights.astype(jnp.bfloat16)).astype(jnp.float32)


def reference(prompt_kv, queries, new_kv, resident_kv, seq_lengths):
    group_size = QH // KVH
    logit_scale_factor = DH ** -0.5
    query_heads = jnp.transpose(queries.reshape(STEPS, SAMPLES, KVH, group_size, DH), (2, 0, 1, 3, 4))
    prompt_keys = jnp.transpose(prompt_kv[0].reshape(PROMPT, KVH, DH), (1, 0, 2))
    prompt_values = jnp.transpose(prompt_kv[1].reshape(PROMPT, KVH, DH), (1, 0, 2))
    resident_keys = jnp.transpose(resident_kv[0].reshape(SAMPLES, RES, KVH, DH), (2, 0, 1, 3))
    resident_values = jnp.transpose(resident_kv[1].reshape(SAMPLES, RES, KVH, DH), (2, 0, 1, 3))
    new_keys = jnp.transpose(new_kv[0].reshape(STEPS, SAMPLES, KVH, DH), (2, 0, 1, 3))
    new_values = jnp.transpose(new_kv[1].reshape(STEPS, SAMPLES, KVH, DH), (2, 0, 1, 3))
    visible = jnp.arange(RES, dtype=jnp.int32)[None, :] < seq_lengths.astype(jnp.int32)[:, None]
    causal = jnp.arange(STEPS, dtype=jnp.int32)[None, :] <= jnp.arange(STEPS, dtype=jnp.int32)[:, None]

    def one_head(head_items):
        query_all, shared_prompt_key, shared_prompt_value, resident_key_rows, resident_value_rows, fresh_key_rows, fresh_value_rows = head_items
        shared_prompt_key = shared_prompt_key.astype(jnp.float32)
        shared_prompt_value = shared_prompt_value.astype(jnp.float32)
        resident_key_rows = resident_key_rows.astype(jnp.float32)
        resident_value_rows = resident_value_rows.astype(jnp.float32)
        fresh_key_rows = fresh_key_rows.astype(jnp.float32)
        fresh_value_rows = fresh_value_rows.astype(jnp.float32)
        results = []
        for step_index in range(STEPS):
            current_step_query = query_all[step_index].astype(jnp.float32)
            shared_prompt_scores = jnp.einsum('jrs,qs->jrq', current_step_query, shared_prompt_key) * logit_scale_factor
            kept_resident_scores = jnp.einsum('qwo,qno->qwn', current_step_query, resident_key_rows) * logit_scale_factor
            kept_resident_scores = jnp.where(visible[:, None, :], kept_resident_scores, MASKED_SCORE)
            fresh_token_scores = jnp.einsum('noh,xnh->nox', current_step_query, fresh_key_rows) * logit_scale_factor
            fresh_token_scores = jnp.where(causal[step_index][None, None, :], fresh_token_scores, MASKED_SCORE)
            row_max = jnp.maximum(jnp.maximum(jnp.max(shared_prompt_scores, axis=-1), jnp.max(kept_resident_scores, axis=-1)), jnp.max(fresh_token_scores, axis=-1))
            shared_prompt_weights = jnp.exp(shared_prompt_scores - row_max[..., None])
            kept_resident_weights = jnp.exp(kept_resident_scores - row_max[..., None])
            fresh_token_weights = jnp.exp(fresh_token_scores - row_max[..., None])
            total = jnp.sum(shared_prompt_weights, axis=-1) + jnp.sum(kept_resident_weights, axis=-1) + jnp.sum(fresh_token_weights, axis=-1)
            blended_output = jnp.einsum('oeb,bg->oeg', lowered_precision_weights(shared_prompt_weights), shared_prompt_value)
            blended_output = blended_output + jnp.einsum('ksj,kjy->ksy', lowered_precision_weights(kept_resident_weights), resident_value_rows)
            blended_output = blended_output + jnp.einsum('gzq,qgf->gzf', lowered_precision_weights(fresh_token_weights), fresh_value_rows)
            results.append((blended_output / total[..., None]).astype(jnp.bfloat16))
        return jnp.stack(results)

    per_head = lax.map(one_head, (query_heads, prompt_keys, prompt_values, resident_keys, resident_values, new_keys, new_values))
    return jnp.transpose(per_head, (1, 2, 0, 3, 4)).reshape(STEPS, SAMPLES, QH * DH)
```

```python
import jax
import jax.numpy as jnp
from jax import lax
from jax.experimental import pallas as pl
from jax.experimental.pallas import tpu as pltpu
from jax.sharding import PartitionSpec as P

DH = 128
STEPS = 3
MASKED_SCORE = -1e30
LOG2E = 1.4426950408889634
SCALE = LOG2E * DH**-0.5
MESH = pl.DeviceIdType.MESH

ROW_TILE = 1024
TOKEN_BLOCK = 256
PIECE = 128
EXTRA = 16
HI, LO = jnp.float32, jnp.bfloat16


def dot_nt(a, b):
    return lax.dot_general(a, b, (((1,), (1,)), ((), ())), preferred_element_type=HI)


def dot_nn(a, b):
    return lax.dot_general(a, b, (((1,), (0,)), ((), ())), preferred_element_type=HI)


def twice(a):
    return jnp.concatenate([a, a], axis=1)


def with_ones(values):
    return jnp.concatenate([values, jnp.ones_like(values)], axis=1)


def absorb(scores, values, state_max, state_out):
    width = scores.shape[1]
    new_max = jnp.maximum(state_max, jnp.max(scores, axis=1, keepdims=True))
    weights = jnp.exp2(scores - jnp.concatenate([new_max] * (width // DH), axis=1))
    mixed = dot_nn(weights.astype(LO), with_ones(values))
    if state_out is not None:
        mixed = state_out * twice(jnp.exp2(state_max - new_max)) + mixed
    return new_max, mixed


def encode_logsum(logsum):
    flat = jnp.transpose(logsum)[0:EXTRA]
    high = flat.astype(LO).astype(HI)
    middle = (flat - high).astype(LO).astype(HI)
    low = flat - high - middle
    row = lax.broadcasted_iota(jnp.int32, (EXTRA, DH), 0)
    return jnp.where(
        row == 0, high, jnp.where(row == 1, middle, jnp.where(row == 2, low, 0.0))
    ).astype(LO)


def decode_logsum(coded):
    parts = coded.astype(HI)
    flat = parts[0:1] + parts[1:2] + parts[2:3]
    return jnp.transpose(jnp.broadcast_to(flat, (PIECE, DH)))


def merge(pieces):
    logsums = [decode_logsum(p[PIECE:]) for p in pieces]
    top = logsums[0]
    for logsum in logsums[1:]:
        top = jnp.maximum(top, logsum)
    shares = [jnp.exp2(logsum - top) for logsum in logsums]
    total = sum(shares[1:], shares[0])
    mixed = None
    for share, piece in zip(shares, pieces):
        term = share * piece[:PIECE].astype(HI)
        mixed = term if mixed is None else mixed + term
    return mixed / total, top + jnp.log(total) * LOG2E


def kernel(
    lengths_ref, prompt_ref, query_ref, new_ref, resident_ref, out_ref,
    own, far, wide, resident, fresh, state_max, state_out,
    part, swapped, joined, crossed,
    local_sems, resident_sems, far_send, far_recv, swap_send, swap_recv,
    cross_send, cross_recv, gather_send, gather_recv, forward_send, forward_recv,
):
    rows = query_ref.shape[0]
    samples = lengths_ref.shape[0]
    blocks = rows // ROW_TILE
    per_sample = rows // samples
    slots = resident_ref.shape[2]
    tokens = prompt_ref.shape[1]
    group = lax.axis_index("group")
    seq = lax.axis_index("seq")
    x, core = seq // 2, lax.rem(seq, 2)
    other_group = {"group": 1 - group}
    other_core = {"seq": 2 * x + 1 - core}
    peers = [lax.rem(x + d, 4) for d in (1, 2, 3)]
    sources = [lax.rem(x + 4 - d, 4) for d in (1, 2, 3)]

    barrier = pltpu.get_barrier_semaphore()
    greeted = [other_group, other_core] + [{"seq": 2 * p + core} for p in peers]
    for device in greeted:
        pl.semaphore_signal(barrier, inc=1, device_id=device, device_id_type=MESH)

    prompt_copy = pltpu.make_async_copy(prompt_ref, own, local_sems.at[0])
    prompt_copy.start()
    fresh_copies = [
        pltpu.make_async_copy(
            new_ref.at[kind, :, pl.ds(pl.multiple_of(seq * 16, 16), 16)],
            fresh.at[kind],
            local_sems.at[1 + kind],
        )
        for kind in (0, 1)
    ]
    for copy in fresh_copies:
        copy.start()
    chunks = resident_sems.shape[0]
    chunk = samples // chunks

    def resident_copy(index):
        return pltpu.make_async_copy(
            resident_ref.at[:, pl.ds(index * chunk, chunk)],
            resident.at[:, pl.ds(index * chunk, chunk)],
            resident_sems.at[index],
        )

    for index in range(chunks):
        resident_copy(index).start()

    pl.semaphore_wait(barrier, len(greeted))
    far_copies = [
        pltpu.make_async_remote_copy(
            src_ref=prompt_ref.at[kind],
            dst_ref=far.at[kind],
            send_sem=far_send.at[kind],
            recv_sem=far_recv.at[kind],
            device_id=other_group,
            device_id_type=MESH,
        )
        for kind in (0, 1)
    ]
    for copy in far_copies:
        copy.start()

    def widen(index, carry):
        at = pl.ds(pl.multiple_of(index * 512, 512), 512)
        scaled = query_ref[at].astype(HI) * SCALE
        high = scaled.astype(LO)
        wide[at] = jnp.concatenate([high, (scaled - high.astype(HI)).astype(LO)], axis=1)
        return carry

    lax.fori_loop(0, rows // 512, widen, 0)
    prompt_copy.wait()

    def prompt_tile(at, source, first):
        queries = wide[at]
        top = jnp.full((ROW_TILE, DH), MASKED_SCORE, HI) if first else state_max[at]
        mixed = None if first else state_out[at]
        for start in range(0, tokens, TOKEN_BLOCK):
            span = pl.ds(start, TOKEN_BLOCK)
            scores = dot_nt(queries, twice(source[0, span]))
            top, mixed = absorb(scores, source[1, span], top, mixed)
        return top, mixed

    def tile_rows(index):
        return pl.ds(pl.multiple_of(index * ROW_TILE, ROW_TILE), ROW_TILE)

    def own_tile(index, carry):
        at = tile_rows(index)
        state_max[at], state_out[at] = prompt_tile(at, own, True)
        return carry

    lax.fori_loop(0, blocks, own_tile, 0)

    for copy in fresh_copies:
        copy.wait()
    new_rows = 16 * per_sample
    at = pl.ds(pl.multiple_of(seq * new_rows, new_rows), new_rows)
    padding = jnp.zeros((DH - STEPS * 16, DH), LO)
    new_keys = jnp.concatenate([fresh[0, t] for t in range(STEPS)] + [padding], axis=0)
    new_values = jnp.concatenate([fresh[1, t] for t in range(STEPS)] + [padding], axis=0)
    scores = dot_nt(wide[at], twice(new_keys))
    row = lax.broadcasted_iota(jnp.int32, scores.shape, 0)
    column = lax.broadcasted_iota(jnp.int32, scores.shape, 1)
    row_sample = row // per_sample
    row_step = (row - row_sample * per_sample) // (per_sample // STEPS)
    seen = (column // 16 <= row_step) & (lax.rem(column, 16) == row_sample)
    scores = jnp.where(seen, scores, MASKED_SCORE)
    state_max[at], state_out[at] = absorb(scores, new_values, state_max[at], state_out[at])

    pair_rows = 2 * per_sample
    row = lax.broadcasted_iota(jnp.int32, (pair_rows, 2 * slots), 0)
    column = lax.broadcasted_iota(jnp.int32, (pair_rows, 2 * slots), 1)
    is_first = row < per_sample
    begin = jnp.where(is_first, 0, slots)

    def resident_pair(index):
        first = 2 * index
        at = pl.ds(pl.multiple_of(index * pair_rows, 32), pair_rows)
        pair = pl.ds(first, 2)
        keys = resident[0, pair].reshape(2 * slots, DH)
        values = resident[1, pair].reshape(2 * slots, DH)
        scores = dot_nt(wide[at], twice(keys))
        here = seq * slots
        one = jnp.minimum(lengths_ref[first] - here, slots)
        two = jnp.minimum(lengths_ref[first + 1] - here, slots) + slots
        seen = (column >= begin) & (column < jnp.where(is_first, one, two))
        scores = jnp.where(seen, scores, MASKED_SCORE)
        return at, absorb(scores, values, state_max[at], state_out[at])

    def resident_step(index, carry):
        results = [resident_pair(index * 4 + u) for u in range(4)]
        for at, (top, mixed) in results:
            state_max[at] = top
            state_out[at] = mixed
        return carry

    steps_per_chunk = chunk // 8
    for index in range(chunks):
        resident_copy(index).wait()
        lax.fori_loop(index * steps_per_chunk, (index + 1) * steps_per_chunk, resident_step, 0)

    for copy in far_copies:
        copy.wait_recv()

    def swap_copy(b):
        return pltpu.make_async_remote_copy(
            src_ref=part.at[b, 1 - core], dst_ref=swapped.at[b],
            send_sem=swap_send.at[b], recv_sem=swap_recv.at[b],
            device_id=other_core, device_id_type=MESH,
        )

    def cross_copy(b, d):
        return pltpu.make_async_remote_copy(
            src_ref=joined.at[b, peers[d]], dst_ref=crossed.at[b, d],
            send_sem=cross_send.at[b, d], recv_sem=cross_recv.at[b, d],
            device_id={"seq": 2 * peers[d] + core}, device_id_type=MESH,
        )

    def piece_rows(b, owner):
        start = b * ROW_TILE + core * (ROW_TILE // 2) + owner * PIECE
        return pl.ds(pl.multiple_of(start, PIECE), PIECE)

    def gather_copy(b, d, owner):
        at = piece_rows(b, owner)
        return pltpu.make_async_remote_copy(
            src_ref=out_ref.at[at], dst_ref=out_ref.at[at],
            send_sem=gather_send.at[b, d], recv_sem=gather_recv.at[b, d],
            device_id={"seq": 2 * peers[d] + core}, device_id_type=MESH,
        )

    def forward_copy(b, half):
        start = b * ROW_TILE + half * (ROW_TILE // 2)
        at = pl.ds(pl.multiple_of(start, ROW_TILE // 2), ROW_TILE // 2)
        return pltpu.make_async_remote_copy(
            src_ref=out_ref.at[at], dst_ref=out_ref.at[at],
            send_sem=forward_send.at[b], recv_sem=forward_recv.at[b],
            device_id=other_core, device_id_type=MESH,
        )

    def far_tile(b):
        top, mixed = prompt_tile(tile_rows(b), far, False)
        total = mixed[:, DH:]
        mean = (mixed[:, :DH] / total).astype(LO)
        logsum = top + jnp.log(total) * LOG2E
        for index in range(ROW_TILE // PIECE):
            span = slice(index * PIECE, (index + 1) * PIECE)
            half, owner = index // 4, index % 4
            part[b, half, owner, 0:PIECE] = mean[span]
            part[b, half, owner, PIECE:] = encode_logsum(logsum[span])
        swap_copy(b).start()

    def join_cores(b):
        swap_copy(b).wait_recv()
        for owner in range(4):
            mean, logsum = merge([part[b, core, owner], swapped[b, owner]])
            joined[b, owner, 0:PIECE] = mean.astype(LO)
            joined[b, owner, PIECE:] = encode_logsum(logsum)
        for d in range(3):
            cross_copy(b, d).start()

    def join_chips(b):
        for d in range(3):
            cross_copy(b, d).wait_recv()
        mean, _ = merge([joined[b, x]] + [crossed[b, d] for d in range(3)])
        out_ref[piece_rows(b, x)] = mean.astype(LO)
        for d in range(3):
            gather_copy(b, d, x).start()

    def forward(b):
        for d in range(3):
            gather_copy(b, d, sources[d]).wait_recv()
        forward_copy(b, core).start()

    def turn(b, carry):
        pl.when(b < blocks)(lambda: far_tile(b))
        pl.when((b >= 1) & (b < blocks + 1))(lambda: join_cores(b - 1))
        pl.when((b >= 2) & (b < blocks + 2))(lambda: join_chips(b - 2))
        pl.when(b >= 3)(lambda: forward(b - 3))
        return carry

    lax.fori_loop(0, blocks + 3, turn, 0)

    for copy in far_copies:
        copy.wait_send()

    def finish(b, carry):
        swap_copy(b).wait_send()
        for d in range(3):
            cross_copy(b, d).wait_send()
            gather_copy(b, d, x).wait_send()
        forward_copy(b, core).wait_send()
        forward_copy(b, 1 - core).wait_recv()
        return carry

    lax.fori_loop(0, blocks, finish, 0)


def local(prompt_kv, queries, new_kv, resident_kv, seq_lengths):
    steps, samples, columns = queries.shape
    heads = columns // DH
    rows = steps * samples * heads
    query_rows = jnp.transpose(queries.reshape(steps, samples, heads, DH), (1, 0, 2, 3))
    query_rows = query_rows.reshape(rows, DH)
    blocks = rows // ROW_TILE
    piece = (PIECE + EXTRA, DH)
    dma = pltpu.SemaphoreType.DMA
    anywhere = pl.BlockSpec(memory_space=pl.ANY)
    in_vmem = pl.BlockSpec(memory_space=pltpu.VMEM)
    out = pl.pallas_call(
        kernel,
        out_shape=jax.ShapeDtypeStruct((rows, DH), LO),
        in_specs=[pl.BlockSpec(memory_space=pltpu.SMEM), anywhere, in_vmem, anywhere, anywhere],
        out_specs=in_vmem,
        scratch_shapes=[
            pltpu.VMEM(prompt_kv.shape, LO),
            pltpu.VMEM(prompt_kv.shape, LO),
            pltpu.VMEM((rows, 2 * DH), LO),
            pltpu.VMEM(resident_kv.shape, LO),
            pltpu.VMEM((2, steps, 16, DH), LO),
            pltpu.VMEM((rows, DH), HI),
            pltpu.VMEM((rows, 2 * DH), HI),
            pltpu.VMEM((blocks, 2, 4) + piece, LO),
            pltpu.VMEM((blocks, 4) + piece, LO),
            pltpu.VMEM((blocks, 4) + piece, LO),
            pltpu.VMEM((blocks, 3) + piece, LO),
            dma((3,)), dma((4,)), dma((2,)), dma((2,)), dma((blocks,)), dma((blocks,)),
            dma((blocks, 3)), dma((blocks, 3)), dma((blocks, 3)), dma((blocks, 3)),
            dma((blocks,)), dma((blocks,)),
        ],
        compiler_params=pltpu.CompilerParams(
            collective_id=0, has_side_effects=True, vmem_limit_bytes=58 * 2**20
        ),
    )(seq_lengths, prompt_kv, query_rows, new_kv, resident_kv)
    out = jnp.transpose(out.reshape(samples, steps, heads, DH), (1, 0, 2, 3))
    return out.reshape(queries.shape)


def solution(mesh):
    placed = (
        P(None, ("group", "seq"), "head"),
        P(None, "group", "head"),
        P(None, None, "group", "head"),
        P(None, "group", "seq", "head"),
        P("group"),
    )
    return jax.shard_map(
        local, mesh=mesh, in_specs=placed, out_specs=P(None, "group", "head"), check_vma=False
    )
```

```python
import jax
import jax.numpy as jnp
from jax import lax
from jax.experimental import pallas as pl
from jax.experimental.pallas import tpu as pltpu
from jax.sharding import PartitionSpec as P

DH = 128
STEPS = 3
MASKED_SCORE = -1e30
LOG2E = 1.4426950408889634
SCALE = LOG2E * DH**-0.5
MESH = pl.DeviceIdType.MESH

ROW_TILE = 1024
OWN_ROWS = 2048
GROUP_ROWS = 256
TOKEN_BLOCK = 1024
LAGS = (1, 3, 5)
PIECE = 128
EXTRA = 16
HI, LO = jnp.float32, jnp.bfloat16


def dot_nt(a, b):
    return lax.dot_general(a, b, (((1,), (1,)), ((), ())), preferred_element_type=HI)


def dot_nn(a, b):
    return lax.dot_general(a, b, (((1,), (0,)), ((), ())), preferred_element_type=HI)


def twice(a):
    return jnp.concatenate([a, a], axis=1)


def with_ones(values):
    return jnp.concatenate([values, jnp.ones_like(values)], axis=1)


def absorb(scores, values, state_max, state_out):
    width = scores.shape[1]
    new_max = jnp.maximum(state_max, jnp.max(scores, axis=1, keepdims=True))
    weights = jnp.exp2(scores - jnp.concatenate([new_max] * (width // DH), axis=1))
    mixed = dot_nn(weights.astype(LO), with_ones(values))
    if state_out is not None:
        mixed = state_out * twice(jnp.exp2(state_max - new_max)) + mixed
    return new_max, mixed


def encode_logsum(logsum):
    flat = jnp.transpose(logsum)[0:EXTRA]
    high = flat.astype(LO).astype(HI)
    middle = (flat - high).astype(LO).astype(HI)
    low = flat - high - middle
    row = lax.broadcasted_iota(jnp.int32, (EXTRA, DH), 0)
    return jnp.where(
        row == 0, high, jnp.where(row == 1, middle, jnp.where(row == 2, low, 0.0))
    ).astype(LO)


def decode_logsum(coded):
    parts = coded.astype(HI)
    flat = parts[0:1] + parts[1:2] + parts[2:3]
    return jnp.transpose(jnp.broadcast_to(flat, (PIECE, DH)))


def merge(pieces):
    logsums = [decode_logsum(p[PIECE:]) for p in pieces]
    top = logsums[0]
    for logsum in logsums[1:]:
        top = jnp.maximum(top, logsum)
    shares = [jnp.exp2(logsum - top) for logsum in logsums]
    total = sum(shares[1:], shares[0])
    mixed = None
    for share, piece in zip(shares, pieces):
        term = share * piece[:PIECE].astype(HI)
        mixed = term if mixed is None else mixed + term
    return mixed / total, top + jnp.log(total) * LOG2E


def kernel(
    lengths_ref, prompt_ref, asked_ref, new_ref, resident_ref, out_ref,
    cached, asked, spread, query_ref, wide, resident, fresh, state_max, state_out,
    part, swapped, joined, crossed,
    local_sems, resident_sems, far_send, far_recv, swap_send, swap_recv,
    cross_send, cross_recv, gather_send, gather_recv, forward_send, forward_recv,
):
    samples = lengths_ref.shape[0]
    rows = query_ref.shape[0]
    blocks = rows // ROW_TILE
    step_rows = rows // STEPS
    heads = step_rows // samples
    slots = resident_ref.shape[2]
    tokens = prompt_ref.shape[1]
    group = lax.axis_index("group")
    seq = lax.axis_index("seq")
    x, core = seq // 2, lax.rem(seq, 2)
    other_group = {"group": 1 - group}
    other_core = {"seq": 2 * x + 1 - core}
    peers = [lax.rem(x + d, 4) for d in (1, 2, 3)]
    sources = [lax.rem(x + 4 - d, 4) for d in (1, 2, 3)]

    barrier = pltpu.get_barrier_semaphore()
    greeted = [other_group, other_core] + [{"seq": 2 * p + core} for p in peers]
    for device in greeted:
        pl.semaphore_signal(barrier, inc=1, device_id=device, device_id_type=MESH)

    prompt_copy = pltpu.make_async_copy(
        prompt_ref, cached.at[:, pl.ds(0, tokens)], local_sems.at[0]
    )
    prompt_copy.start()
    asked_copy = pltpu.make_async_copy(asked_ref, asked, local_sems.at[3])
    asked_copy.start()
    fresh_copies = [
        pltpu.make_async_copy(
            new_ref.at[kind, :, pl.ds(pl.multiple_of(seq * 16, 16), 16)],
            fresh.at[kind],
            local_sems.at[1 + kind],
        )
        for kind in (0, 1)
    ]
    for copy in fresh_copies:
        copy.start()
    chunks = resident_sems.shape[0]
    chunk = samples // chunks

    def resident_copy(index):
        return pltpu.make_async_copy(
            resident_ref.at[:, pl.ds(index * chunk, chunk)],
            resident.at[:, pl.ds(index * chunk, chunk)],
            resident_sems.at[index],
        )

    for index in range(chunks):
        resident_copy(index).start()

    def tile_rows(index):
        return pl.ds(pl.multiple_of(index * ROW_TILE, ROW_TILE), ROW_TILE)

    def clear(index, carry):
        state_max[tile_rows(index)] = jnp.full((ROW_TILE, DH), MASKED_SCORE, HI)
        state_out[tile_rows(index)] = jnp.zeros((ROW_TILE, 2 * DH), HI)
        return carry

    lax.fori_loop(0, blocks, clear, 0)

    pl.semaphore_wait(barrier, len(greeted))
    far_copies = [
        pltpu.make_async_remote_copy(
            src_ref=prompt_ref.at[kind],
            dst_ref=cached.at[kind, pl.ds(tokens, tokens)],
            send_sem=far_send.at[kind],
            recv_sem=far_recv.at[kind],
            device_id=other_group,
            device_id_type=MESH,
        )
        for kind in (0, 1)
    ]
    for copy in far_copies:
        copy.start()

    asked_copy.wait()

    def widen(index, carry):
        step, first = index // (samples // 16), 16 * lax.rem(index, samples // 16)
        base = pl.multiple_of(index * 16 * heads, 16 * heads)
        for head in range(heads):
            block = asked[step, pl.ds(pl.multiple_of(first, 16), 16), head * DH : (head + 1) * DH]
            spread[pl.ds(base + head, 16, stride=heads)] = block.astype(HI)
        at = pl.ds(base, 16 * heads)
        plain = spread[at]
        query_ref[at] = plain.astype(LO)
        scaled = plain * SCALE
        high = scaled.astype(LO)
        wide[at] = jnp.concatenate([high, (scaled - high.astype(HI)).astype(LO)], axis=1)
        return carry

    lax.fori_loop(0, STEPS * samples // 16, widen, 0)
    prompt_copy.wait()

    def prompt_rows(begin, count, source):
        groups = [
            pl.ds(pl.multiple_of(begin + offset, GROUP_ROWS), GROUP_ROWS)
            for offset in range(0, count, GROUP_ROWS)
        ]
        state = [(state_max[at], state_out[at]) for at in groups]
        spans = [pl.ds(source * tokens + t, TOKEN_BLOCK) for t in range(0, tokens, TOKEN_BLOCK)]
        order = [(span, g) for span in spans for g in range(len(groups))]

        def scores_of(span, g):
            return dot_nt(wide[groups[g]], twice(cached[0, span]))

        following = scores_of(*order[0])
        for turn_index, (span, g) in enumerate(order):
            scores = following
            if turn_index + 1 < len(order):
                following = scores_of(*order[turn_index + 1])
            state[g] = absorb(scores, cached[1, span], *state[g])
        for at, (top, mixed) in zip(groups, state):
            state_max[at], state_out[at] = top, mixed

    def own_step(index, carry):
        prompt_rows(index * OWN_ROWS, OWN_ROWS, 0)
        return carry

    lax.fori_loop(0, rows // OWN_ROWS, own_step, 0)

    def gather_rows(ref, start, count):
        return jnp.concatenate(
            [ref[pl.ds(start + s * step_rows, count)] for s in range(STEPS)], axis=0
        )

    def scatter_rows(ref, start, count, value):
        for s in range(STEPS):
            ref[pl.ds(start + s * step_rows, count)] = value[s * count : (s + 1) * count]

    for copy in fresh_copies:
        copy.wait()
    new_rows = 16 * heads
    start = pl.multiple_of(seq * new_rows, new_rows)
    padding = jnp.zeros((DH - STEPS * 16, DH), LO)
    new_keys = jnp.concatenate([fresh[0, t] for t in range(STEPS)] + [padding], axis=0)
    new_values = jnp.concatenate([fresh[1, t] for t in range(STEPS)] + [padding], axis=0)
    scores = dot_nt(gather_rows(query_ref, start, new_rows), new_keys) * SCALE
    row = lax.broadcasted_iota(jnp.int32, scores.shape, 0)
    column = lax.broadcasted_iota(jnp.int32, scores.shape, 1)
    row_sample = lax.rem(row, new_rows) // heads
    seen = (column // 16 <= row // new_rows) & (lax.rem(column, 16) == row_sample)
    scores = jnp.where(seen, scores, MASKED_SCORE)
    top, mixed = absorb(
        scores, new_values, gather_rows(state_max, start, new_rows),
        gather_rows(state_out, start, new_rows),
    )
    scatter_rows(state_max, start, new_rows, top)
    scatter_rows(state_out, start, new_rows, mixed)

    pair_rows = 2 * heads
    shape = (STEPS * pair_rows, 2 * slots)
    column = lax.broadcasted_iota(jnp.int32, shape, 1)
    is_first = lax.rem(lax.broadcasted_iota(jnp.int32, shape, 0), pair_rows) < heads
    begin = jnp.where(is_first, 0, slots)

    def pair_scores(index):
        first = 2 * index
        start = pl.multiple_of(index * pair_rows, pair_rows)
        keys = resident[0, pl.ds(first, 2)].reshape(2 * slots, DH)
        scores = dot_nt(gather_rows(query_ref, start, pair_rows), keys) * SCALE
        here = seq * slots
        one = jnp.minimum(lengths_ref[first] - here, slots)
        two = jnp.minimum(lengths_ref[first + 1] - here, slots) + slots
        seen = (column >= begin) & (column < jnp.where(is_first, one, two))
        return jnp.where(seen, scores, MASKED_SCORE)

    def pair_weights(index, scores):
        start = pl.multiple_of(index * pair_rows, pair_rows)
        old = gather_rows(state_max, start, pair_rows)
        top = jnp.maximum(old, jnp.max(scores, axis=1, keepdims=True))
        return top, jnp.exp2(scores - twice(top)).astype(LO), jnp.exp2(old - top)

    def pair_mix(index, weights, decay):
        start = pl.multiple_of(index * pair_rows, pair_rows)
        values = resident[1, pl.ds(2 * index, 2)].reshape(2 * slots, DH)
        mixed = dot_nn(weights, with_ones(values))
        return gather_rows(state_out, start, pair_rows) * twice(decay) + mixed

    pairs = chunk // 2

    def resident_step(step, carry):
        resident_copy(step).wait()
        indices = [step * pairs + u for u in range(pairs)]
        scores = [pair_scores(index) for index in indices]
        weighed = [pair_weights(index, s) for index, s in zip(indices, scores)]
        mixes = [pair_mix(index, w[1], w[2]) for index, w in zip(indices, weighed)]
        for index, (top, _, _), mixed in zip(indices, weighed, mixes):
            start = pl.multiple_of(index * pair_rows, pair_rows)
            scatter_rows(state_max, start, pair_rows, top)
            scatter_rows(state_out, start, pair_rows, mixed)
        return carry

    lax.fori_loop(0, chunks, resident_step, 0)

    for copy in far_copies:
        copy.wait_recv()

    def swap_copy(b):
        return pltpu.make_async_remote_copy(
            src_ref=part.at[b, 1 - core], dst_ref=swapped.at[b],
            send_sem=swap_send.at[b], recv_sem=swap_recv.at[b],
            device_id=other_core, device_id_type=MESH,
        )

    def cross_copy(b, d):
        return pltpu.make_async_remote_copy(
            src_ref=joined.at[b, peers[d]], dst_ref=crossed.at[b, d],
            send_sem=cross_send.at[b, d], recv_sem=cross_recv.at[b, d],
            device_id={"seq": 2 * peers[d] + core}, device_id_type=MESH,
        )

    def piece_rows(b, owner):
        start = b * ROW_TILE + core * (ROW_TILE // 2) + owner * PIECE
        return pl.ds(pl.multiple_of(start, PIECE), PIECE)

    def gather_copy(b, d, owner):
        at = piece_rows(b, owner)
        return pltpu.make_async_remote_copy(
            src_ref=out_ref.at[at], dst_ref=out_ref.at[at],
            send_sem=gather_send.at[b, d], recv_sem=gather_recv.at[b, d],
            device_id={"seq": 2 * peers[d] + core}, device_id_type=MESH,
        )

    def forward_copy(b, half):
        start = b * ROW_TILE + half * (ROW_TILE // 2)
        at = pl.ds(pl.multiple_of(start, ROW_TILE // 2), ROW_TILE // 2)
        return pltpu.make_async_remote_copy(
            src_ref=out_ref.at[at], dst_ref=out_ref.at[at],
            send_sem=forward_send.at[b], recv_sem=forward_recv.at[b],
            device_id=other_core, device_id_type=MESH,
        )

    def far_tile(b):
        prompt_rows(b * ROW_TILE, ROW_TILE, 1)
        top, mixed = state_max[tile_rows(b)], state_out[tile_rows(b)]
        total = mixed[:, DH:]
        mean = (mixed[:, :DH] / total).astype(LO)
        logsum = top + jnp.log(total) * LOG2E
        for index in range(ROW_TILE // PIECE):
            span = slice(index * PIECE, (index + 1) * PIECE)
            side, owner = index // 4, index % 4
            part[b, side, owner, 0:PIECE] = mean[span]
            part[b, side, owner, PIECE:] = encode_logsum(logsum[span])
        swap_copy(b).start()

    def join_cores(b):
        swap_copy(b).wait_recv()
        for owner in range(4):
            mean, logsum = merge([part[b, core, owner], swapped[b, owner]])
            joined[b, owner, 0:PIECE] = mean.astype(LO)
            joined[b, owner, PIECE:] = encode_logsum(logsum)
        for d in range(3):
            cross_copy(b, d).start()

    def join_chips(b):
        for d in range(3):
            cross_copy(b, d).wait_recv()
        mean, _ = merge([joined[b, x]] + [crossed[b, d] for d in range(3)])
        out_ref[piece_rows(b, x)] = mean.astype(LO)
        for d in range(3):
            gather_copy(b, d, x).start()

    def forward(b):
        for d in range(3):
            gather_copy(b, d, sources[d]).wait_recv()
        forward_copy(b, core).start()

    def turn(b, carry):
        pl.when(b < blocks)(lambda: far_tile(b))
        late, later, last = (b - lag for lag in LAGS)
        pl.when((late >= 0) & (late < blocks))(lambda: join_cores(late))
        pl.when((later >= 0) & (later < blocks))(lambda: join_chips(later))
        pl.when(last >= 0)(lambda: forward(last))
        return carry

    lax.fori_loop(0, blocks + LAGS[2], turn, 0)

    for copy in far_copies:
        copy.wait_send()

    def finish(b, carry):
        swap_copy(b).wait_send()
        for d in range(3):
            cross_copy(b, d).wait_send()
            gather_copy(b, d, x).wait_send()
        forward_copy(b, core).wait_send()
        forward_copy(b, 1 - core).wait_recv()
        return carry

    lax.fori_loop(0, blocks, finish, 0)


def local(prompt_kv, queries, new_kv, resident_kv, seq_lengths):
    steps, samples, columns = queries.shape
    heads = columns // DH
    rows = steps * samples * heads
    blocks = rows // ROW_TILE
    piece = (PIECE + EXTRA, DH)
    dma = pltpu.SemaphoreType.DMA
    anywhere = pl.BlockSpec(memory_space=pl.ANY)
    in_vmem = pl.BlockSpec(memory_space=pltpu.VMEM)
    out = pl.pallas_call(
        kernel,
        out_shape=jax.ShapeDtypeStruct((rows, DH), LO),
        in_specs=[pl.BlockSpec(memory_space=pltpu.SMEM), anywhere, anywhere, anywhere, anywhere],
        out_specs=in_vmem,
        scratch_shapes=[
            pltpu.VMEM((2, 2 * prompt_kv.shape[1], DH), LO),
            pltpu.VMEM(queries.shape, LO),
            pltpu.VMEM((rows, DH), HI),
            pltpu.VMEM((rows, DH), LO),
            pltpu.VMEM((rows, 2 * DH), LO),
            pltpu.VMEM(resident_kv.shape, LO),
            pltpu.VMEM((2, steps, 16, DH), LO),
            pltpu.VMEM((rows, DH), HI),
            pltpu.VMEM((rows, 2 * DH), HI),
            pltpu.VMEM((blocks, 2, 4) + piece, LO),
            pltpu.VMEM((blocks, 4) + piece, LO),
            pltpu.VMEM((blocks, 4) + piece, LO),
            pltpu.VMEM((blocks, 3) + piece, LO),
            dma((4,)), dma((4,)), dma((2,)), dma((2,)), dma((blocks,)), dma((blocks,)),
            dma((blocks, 3)), dma((blocks, 3)), dma((blocks, 3)), dma((blocks, 3)),
            dma((blocks,)), dma((blocks,)),
        ],
        compiler_params=pltpu.CompilerParams(
            collective_id=0, has_side_effects=True, vmem_limit_bytes=48 * 2**20
        ),
    )(seq_lengths, prompt_kv, queries, new_kv, resident_kv)
    return out.reshape(queries.shape)


def solution(mesh):
    placed = (
        P(None, ("group", "seq"), "head"),
        P(None, "group", "head"),
        P(None, None, "group", "head"),
        P(None, "group", "seq", "head"),
        P("group"),
    )
    return jax.shard_map(
        local, mesh=mesh, in_specs=placed, out_specs=P(None, "group", "head"), check_vma=False
    )
```

```python
import jax
import jax.numpy as jnp
from jax import lax
from jax.experimental import pallas as pl
from jax.experimental.pallas import tpu as pltpu
from jax.sharding import PartitionSpec as P

DH = 128
STEPS = 3
MASKED_SCORE = -1e30
LOG2E = 1.4426950408889634
SCALE = LOG2E * DH**-0.5
MESH = pl.DeviceIdType.MESH

ROW_TILE = 512
OWN_ROWS = 1536
GROUP_ROWS = 256
TOKEN_BLOCK = 1024
EARLY = 2
LAGS = (2, 3)
PIECE = 128
EXTRA = 16
HI, LO = jnp.float32, jnp.bfloat16


def dot_nt(a, b):
    return lax.dot_general(a, b, (((1,), (1,)), ((), ())), preferred_element_type=HI)


def dot_nn(a, b):
    return lax.dot_general(a, b, (((1,), (0,)), ((), ())), preferred_element_type=HI)


def twice(a):
    return jnp.concatenate([a, a], axis=1)


def with_ones(values):
    return jnp.concatenate([values, jnp.ones_like(values)], axis=1)


def absorb(scores, values, state_max, state_out):
    width = scores.shape[1]
    new_max = jnp.maximum(state_max, jnp.max(scores, axis=1, keepdims=True))
    weights = jnp.exp2(scores - jnp.concatenate([new_max] * (width // DH), axis=1))
    mixed = dot_nn(weights.astype(LO), with_ones(values))
    if state_out is not None:
        mixed = state_out * twice(jnp.exp2(state_max - new_max)) + mixed
    return new_max, mixed


def on_diagonal():
    row = lax.broadcasted_iota(jnp.int32, (PIECE, DH), 0)
    return row == lax.broadcasted_iota(jnp.int32, (PIECE, DH), 1)


def encode_logsum(logsum):
    flat = jnp.sum(jnp.where(on_diagonal(), logsum, 0.0), axis=0, keepdims=True)
    flat = jnp.broadcast_to(flat, (EXTRA, DH))
    high = flat.astype(LO).astype(HI)
    middle = (flat - high).astype(LO).astype(HI)
    low = flat - high - middle
    row = lax.broadcasted_iota(jnp.int32, (EXTRA, DH), 0)
    return jnp.where(
        row == 0, high, jnp.where(row == 1, middle, jnp.where(row == 2, low, 0.0))
    ).astype(LO)


def decode_logsum(coded):
    parts = coded.astype(HI)
    flat = parts[0:1] + parts[1:2] + parts[2:3]
    own = jnp.where(on_diagonal(), jnp.broadcast_to(flat, (PIECE, DH)), 0.0)
    return jnp.broadcast_to(jnp.sum(own, axis=1, keepdims=True), (PIECE, DH))


def merge(pieces):
    logsums = [decode_logsum(p[PIECE:]) for p in pieces]
    top = logsums[0]
    for logsum in logsums[1:]:
        top = jnp.maximum(top, logsum)
    shares = [jnp.exp2(logsum - top) for logsum in logsums]
    total = sum(shares[1:], shares[0])
    mixed = None
    for share, piece in zip(shares, pieces):
        term = share * piece[:PIECE].astype(HI)
        mixed = term if mixed is None else mixed + term
    return mixed / total, top + jnp.log(total) * LOG2E


def kernel(
    lengths_ref, prompt_ref, asked_ref, new_ref, resident_ref, out_ref,
    cached, asked, spread, query_ref, wide, resident, fresh, state_max, state_out,
    part, swapped, joined, crossed,
    local_sems, resident_sems, near_send, near_recv, far_send, far_recv,
    relay_send, relay_recv, swap_send, swap_recv,
    cross_send, cross_recv, gather_send, gather_recv, forward_send, forward_recv,
    last_send, last_recv,
):
    samples = lengths_ref.shape[0]
    rows = query_ref.shape[0]
    core_rows = rows // 2
    blocks = core_rows // ROW_TILE
    step_rows = rows // STEPS
    heads = step_rows // samples
    slots = resident_ref.shape[2]
    tokens = prompt_ref.shape[1]
    group = lax.axis_index("group")
    seq = lax.axis_index("seq")
    x, core = seq // 2, lax.rem(seq, 2)
    core_start = core * core_rows
    other_group = {"group": 1 - group}
    other_core = {"seq": 2 * x + 1 - core}
    peers = [lax.rem(x + d, 4) for d in (1, 2, 3)]
    sources = [lax.rem(x + 4 - d, 4) for d in (1, 2, 3)]

    barrier = pltpu.get_barrier_semaphore()
    greeted = [other_group, other_core] + [
        {"seq": 2 * p + side} for p in peers for side in (0, 1)
    ]
    for device in greeted:
        pl.semaphore_signal(barrier, inc=1, device_id=device, device_id_type=MESH)

    prompt_copy = pltpu.make_async_copy(
        prompt_ref, cached.at[:, pl.ds(0, tokens)], local_sems.at[0]
    )
    prompt_copy.start()
    asked_copy = pltpu.make_async_copy(asked_ref, asked, local_sems.at[3])
    asked_copy.start()
    fresh_copies = [
        pltpu.make_async_copy(
            new_ref.at[kind, :, pl.ds(pl.multiple_of(seq * 16, 16), 16)],
            fresh.at[kind],
            local_sems.at[1 + kind],
        )
        for kind in (0, 1)
    ]
    for copy in fresh_copies:
        copy.start()
    chunks = resident_sems.shape[0]
    chunk = samples // chunks

    def resident_copy(index):
        return pltpu.make_async_copy(
            resident_ref.at[:, pl.ds(index * chunk, chunk)],
            resident.at[:, pl.ds(index * chunk, chunk)],
            resident_sems.at[index],
        )

    for index in range(chunks):
        resident_copy(index).start()

    def clear(index, carry):
        at = pl.ds(pl.multiple_of(index * 512, 512), 512)
        state_max[at] = jnp.full((512, DH), MASKED_SCORE, HI)
        state_out[at] = jnp.zeros((512, 2 * DH), HI)
        return carry

    lax.fori_loop(0, rows // 512, clear, 0)

    pl.semaphore_wait(barrier, len(greeted))
    def token_copies(source, source_start, start, send, recv, device):
        return [
            pltpu.make_async_remote_copy(
                src_ref=source.at[kind, pl.ds(source_start, tokens)],
                dst_ref=cached.at[kind, pl.ds(start, tokens)],
                send_sem=send.at[kind],
                recv_sem=recv.at[kind],
                device_id=device,
                device_id_type=MESH,
            )
            for kind in (0, 1)
        ]

    far_copies = token_copies(prompt_ref, 0, 2 * tokens, far_send, far_recv, other_group)
    near_copies = token_copies(prompt_ref, 0, tokens, near_send, near_recv, other_core)
    relay_copies = token_copies(
        cached, 2 * tokens, 3 * tokens, relay_send, relay_recv, other_core
    )
    for copy in far_copies + near_copies:
        copy.start()

    asked_copy.wait()

    def widen(index, carry):
        step, first = index // (samples // 16), 16 * lax.rem(index, samples // 16)
        base = pl.multiple_of(index * 16 * heads, 16 * heads)
        for head in range(heads):
            block = asked[step, pl.ds(pl.multiple_of(first, 16), 16), head * DH : (head + 1) * DH]
            spread[pl.ds(base + head, 16, stride=heads)] = block.astype(HI)
        at = pl.ds(base, 16 * heads)
        plain = spread[at]
        query_ref[at] = plain.astype(LO)
        scaled = plain * SCALE
        high = scaled.astype(LO)
        wide[at] = jnp.concatenate([high, (scaled - high.astype(HI)).astype(LO)], axis=1)
        return carry

    lax.fori_loop(0, STEPS * samples // 16, widen, 0)

    def gather_rows(ref, start, count):
        return jnp.concatenate(
            [ref[pl.ds(start + s * step_rows, count)] for s in range(STEPS)], axis=0
        )

    def scatter_rows(ref, start, count, value):
        for s in range(STEPS):
            ref[pl.ds(start + s * step_rows, count)] = value[s * count : (s + 1) * count]

    for copy in fresh_copies:
        copy.wait()
    new_rows = 16 * heads
    start = pl.multiple_of(seq * new_rows, new_rows)
    padding = jnp.zeros((DH - STEPS * 16, DH), LO)
    new_keys = jnp.concatenate([fresh[0, t] for t in range(STEPS)] + [padding], axis=0)
    new_values = jnp.concatenate([fresh[1, t] for t in range(STEPS)] + [padding], axis=0)
    scores = dot_nt(gather_rows(query_ref, start, new_rows), new_keys) * SCALE
    row = lax.broadcasted_iota(jnp.int32, scores.shape, 0)
    column = lax.broadcasted_iota(jnp.int32, scores.shape, 1)
    row_sample = lax.rem(row, new_rows) // heads
    seen = (column // 16 <= row // new_rows) & (lax.rem(column, 16) == row_sample)
    scores = jnp.where(seen, scores, MASKED_SCORE)
    top, mixed = absorb(
        scores, new_values, gather_rows(state_max, start, new_rows),
        gather_rows(state_out, start, new_rows),
    )
    scatter_rows(state_max, start, new_rows, top)
    scatter_rows(state_out, start, new_rows, mixed)

    pair_rows = 2 * heads
    shape = (STEPS * pair_rows, 2 * slots)
    column = lax.broadcasted_iota(jnp.int32, shape, 1)
    is_first = lax.rem(lax.broadcasted_iota(jnp.int32, shape, 0), pair_rows) < heads
    begin = jnp.where(is_first, 0, slots)

    def pair_scores(index):
        first = 2 * index
        start = pl.multiple_of(index * pair_rows, pair_rows)
        keys = resident[0, pl.ds(first, 2)].reshape(2 * slots, DH)
        scores = dot_nt(gather_rows(query_ref, start, pair_rows), keys) * SCALE
        here = seq * slots
        one = jnp.minimum(lengths_ref[first] - here, slots)
        two = jnp.minimum(lengths_ref[first + 1] - here, slots) + slots
        seen = (column >= begin) & (column < jnp.where(is_first, one, two))
        return jnp.where(seen, scores, MASKED_SCORE)

    def pair_weights(index, scores):
        start = pl.multiple_of(index * pair_rows, pair_rows)
        old = gather_rows(state_max, start, pair_rows)
        top = jnp.maximum(old, jnp.max(scores, axis=1, keepdims=True))
        return top, jnp.exp2(scores - twice(top)).astype(LO), jnp.exp2(old - top)

    def pair_mix(index, weights, decay):
        start = pl.multiple_of(index * pair_rows, pair_rows)
        values = resident[1, pl.ds(2 * index, 2)].reshape(2 * slots, DH)
        mixed = dot_nn(weights, with_ones(values))
        return gather_rows(state_out, start, pair_rows) * twice(decay) + mixed

    pairs = chunk // 2

    def resident_step(step, carry):
        resident_copy(step).wait()
        indices = [step * pairs + u for u in range(pairs)]
        scores = [pair_scores(index) for index in indices]
        weighed = [pair_weights(index, s) for index, s in zip(indices, scores)]
        mixes = [pair_mix(index, w[1], w[2]) for index, w in zip(indices, weighed)]
        for index, (top, _, _), mixed in zip(indices, weighed, mixes):
            start = pl.multiple_of(index * pair_rows, pair_rows)
            scatter_rows(state_max, start, pair_rows, top)
            scatter_rows(state_out, start, pair_rows, mixed)
        return carry

    lax.fori_loop(0, chunks, resident_step, 0)

    def piece_state(at):
        total = state_out[at, DH:]
        return state_out[at, :DH] / total, state_max[at] + jnp.log(total) * LOG2E

    def pack_step(index, carry):
        for u in range(4):
            start = (core_rows - core_start) + (4 * index + u) * PIECE
            mean, logsum = piece_state(pl.ds(pl.multiple_of(start, PIECE), PIECE))
            part[4 * index + u, 0:PIECE] = mean.astype(LO)
            part[4 * index + u, PIECE:] = encode_logsum(logsum)
        return carry

    lax.fori_loop(0, blocks, pack_step, 0)
    swap_copy = pltpu.make_async_remote_copy(
        src_ref=part, dst_ref=swapped, send_sem=swap_send, recv_sem=swap_recv,
        device_id=other_core, device_id_type=MESH,
    )
    swap_copy.start()

    def prompt_rows(begin, count, first, length):
        groups = [
            pl.ds(pl.multiple_of(begin + offset, GROUP_ROWS), GROUP_ROWS)
            for offset in range(0, count, GROUP_ROWS)
        ]
        state = [(state_max[at], state_out[at]) for at in groups]
        spans = [pl.ds(t, TOKEN_BLOCK) for t in range(first, first + length, TOKEN_BLOCK)]
        order = [(span, g) for span in spans for g in range(len(groups))]

        def scores_of(span, g):
            return dot_nt(wide[groups[g]], twice(cached[0, span]))

        following = scores_of(*order[0])
        for turn_index, (span, g) in enumerate(order):
            scores = following
            if turn_index + 1 < len(order):
                following = scores_of(*order[turn_index + 1])
            state[g] = absorb(scores, cached[1, span], *state[g])
        for at, (top, mixed) in zip(groups, state):
            state_max[at], state_out[at] = top, mixed

    def own_step(index, carry):
        prompt_rows(core_start + index * OWN_ROWS, OWN_ROWS, 0, 2 * tokens)
        return carry

    prompt_copy.wait()
    for copy in near_copies:
        copy.wait_recv()
    lax.fori_loop(0, core_rows // OWN_ROWS, own_step, 0)
    swap_copy.wait_recv()
    for far_copy, relay_copy in zip(far_copies, relay_copies):
        far_copy.wait_recv()
        relay_copy.start()

    def early_step(b, carry):
        prompt_rows(core_start + b * ROW_TILE, ROW_TILE, 2 * tokens, tokens)
        return carry

    lax.fori_loop(0, EARLY, early_step, 0)
    for relay_copy in relay_copies:
        relay_copy.wait_recv()

    def cross_copy(b, d):
        return pltpu.make_async_remote_copy(
            src_ref=joined.at[b, peers[d]], dst_ref=crossed.at[b, d],
            send_sem=cross_send.at[b, d], recv_sem=cross_recv.at[b, d],
            device_id={"seq": 2 * peers[d] + core}, device_id_type=MESH,
        )

    def piece_rows(b, owner):
        start = core_start + b * ROW_TILE + owner * PIECE
        return pl.ds(pl.multiple_of(start, PIECE), PIECE)

    def gather_copy(b, d, owner):
        at = piece_rows(b, owner)
        return pltpu.make_async_remote_copy(
            src_ref=out_ref.at[at], dst_ref=out_ref.at[at],
            send_sem=gather_send.at[b, d], recv_sem=gather_recv.at[b, d],
            device_id={"seq": 2 * peers[d] + core}, device_id_type=MESH,
        )

    def last_copy(d, owner):
        at = piece_rows(blocks - 1, owner)
        target = 2 * (x if d == 3 else peers[d]) + 1 - core
        return pltpu.make_async_remote_copy(
            src_ref=out_ref.at[at], dst_ref=out_ref.at[at],
            send_sem=last_send.at[d], recv_sem=last_recv.at[d],
            device_id={"seq": target}, device_id_type=MESH,
        )

    def forward_copy(b, side):
        start = side * core_rows + b * ROW_TILE
        at = pl.ds(pl.multiple_of(start, ROW_TILE), ROW_TILE)
        return pltpu.make_async_remote_copy(
            src_ref=out_ref.at[at], dst_ref=out_ref.at[at],
            send_sem=forward_send.at[b], recv_sem=forward_recv.at[b],
            device_id=other_core, device_id_type=MESH,
        )

    def far_tile(b):
        begin = core_start + b * ROW_TILE

        @pl.when(b < EARLY)
        def _():
            prompt_rows(begin, ROW_TILE, 3 * tokens, tokens)

        @pl.when(b >= EARLY)
        def _():
            prompt_rows(begin, ROW_TILE, 2 * tokens, 2 * tokens)

        for owner in range(4):
            at = piece_rows(b, owner)
            other = swapped[4 * b + owner]
            other_logsum = decode_logsum(other[PIECE:])
            top = jnp.maximum(state_max[at], other_logsum)
            decay, share = jnp.exp2(state_max[at] - top), jnp.exp2(other_logsum - top)
            total = state_out[at, DH:] * decay + share
            mixed = state_out[at, :DH] * decay + other[:PIECE].astype(HI) * share
            joined[b, owner, 0:PIECE] = (mixed / total).astype(LO)
            joined[b, owner, PIECE:] = encode_logsum(top + jnp.log(total) * LOG2E)
        for d in range(3):
            cross_copy(b, d).start()

    def join_chips(b):
        for d in range(3):
            cross_copy(b, d).wait_recv()
        mean, _ = merge([joined[b, x]] + [crossed[b, d] for d in range(3)])
        out_ref[piece_rows(b, x)] = mean.astype(LO)
        for d in range(3):
            gather_copy(b, d, x).start()

        @pl.when(b == blocks - 1)
        def _():
            for d in range(4):
                last_copy(d, x).start()

    def forward(b):
        for d in range(3):
            gather_copy(b, d, sources[d]).wait_recv()
        pl.when(b < blocks - 1)(lambda: forward_copy(b, core).start())

    def turn(b, carry):
        pl.when(b < blocks)(lambda: far_tile(b))
        late, last = (b - lag for lag in LAGS)
        pl.when((late >= 0) & (late < blocks))(lambda: join_chips(late))
        pl.when(last >= 0)(lambda: forward(last))
        return carry

    lax.fori_loop(0, blocks + LAGS[1], turn, 0)

    for copy in far_copies + near_copies + relay_copies + [swap_copy]:
        copy.wait_send()

    def finish(b, carry):
        for d in range(3):
            cross_copy(b, d).wait_send()
            gather_copy(b, d, x).wait_send()

        @pl.when(b < blocks - 1)
        def _():
            forward_copy(b, core).wait_send()
            forward_copy(b, 1 - core).wait_recv()

        return carry

    lax.fori_loop(0, blocks, finish, 0)
    for d in range(4):
        last_copy(d, x).wait_send()
        at = pl.ds(
            pl.multiple_of(core_rows - core_start + (blocks - 1) * ROW_TILE, PIECE), ROW_TILE
        )
        owner = x if d == 3 else sources[d]
        piece = out_ref.at[at].at[pl.ds(pl.multiple_of(owner * PIECE, PIECE), PIECE)]
        pltpu.make_async_remote_copy(
            src_ref=piece, dst_ref=piece, send_sem=last_send.at[d], recv_sem=last_recv.at[d],
            device_id=other_core, device_id_type=MESH,
        ).wait_recv()


def local(prompt_kv, queries, new_kv, resident_kv, seq_lengths):
    steps, samples, columns = queries.shape
    heads = columns // DH
    rows = steps * samples * heads
    blocks = rows // 2 // ROW_TILE
    piece = (PIECE + EXTRA, DH)
    dma = pltpu.SemaphoreType.DMA
    anywhere = pl.BlockSpec(memory_space=pl.ANY)
    in_vmem = pl.BlockSpec(memory_space=pltpu.VMEM)
    out = pl.pallas_call(
        kernel,
        out_shape=jax.ShapeDtypeStruct((rows, DH), LO),
        in_specs=[pl.BlockSpec(memory_space=pltpu.SMEM), anywhere, anywhere, anywhere, anywhere],
        out_specs=in_vmem,
        scratch_shapes=[
            pltpu.VMEM((2, 4 * prompt_kv.shape[1], DH), LO),
            pltpu.VMEM(queries.shape, LO),
            pltpu.VMEM((rows, DH), HI),
            pltpu.VMEM((rows, DH), LO),
            pltpu.VMEM((rows, 2 * DH), LO),
            pltpu.VMEM(resident_kv.shape, LO),
            pltpu.VMEM((2, steps, 16, DH), LO),
            pltpu.VMEM((rows, DH), HI),
            pltpu.VMEM((rows, 2 * DH), HI),
            pltpu.VMEM((4 * blocks,) + piece, LO),
            pltpu.VMEM((4 * blocks,) + piece, LO),
            pltpu.VMEM((blocks, 4) + piece, LO),
            pltpu.VMEM((blocks, 3) + piece, LO),
            dma((4,)), dma((4,)), dma((2,)), dma((2,)), dma((2,)), dma((2,)),
            dma((2,)), dma((2,)), dma, dma,
            dma((blocks, 3)), dma((blocks, 3)), dma((blocks, 3)), dma((blocks, 3)),
            dma((blocks,)), dma((blocks,)), dma((4,)), dma((4,)),
        ],
        compiler_params=pltpu.CompilerParams(
            collective_id=0, has_side_effects=True, vmem_limit_bytes=48 * 2**20
        ),
    )(seq_lengths, prompt_kv, queries, new_kv, resident_kv)
    return out.reshape(queries.shape)


def solution(mesh):
    placed = (
        P(None, ("group", "seq"), "head"),
        P(None, "group", "head"),
        P(None, None, "group", "head"),
        P(None, "group", "seq", "head"),
        P("group"),
    )
    return jax.shard_map(
        local, mesh=mesh, in_specs=placed, out_specs=P(None, "group", "head"), check_vma=False
    )
```

```python
import jax
import jax.numpy as jnp
from jax import lax
from jax.experimental import pallas as pl
from jax.experimental.pallas import tpu as pltpu
from jax.sharding import PartitionSpec as P

DH = 128
STEPS = 3
MASKED_SCORE = -1e30
LOG2E = 1.4426950408889634
SCALE = LOG2E * DH**-0.5
MESH = pl.DeviceIdType.MESH

ROW_TILE = 512
OWN_ROWS = 1536
GROUP_ROWS = 256
TOKEN_BLOCK = 1024
FARTHEST_FIRST = (1, 0, 2)
EARLY = 2
LAGS = (2, 3)
PIECE = 128
EXTRA = 16
HI, LO = jnp.float32, jnp.bfloat16


def dot_nt(a, b):
    return lax.dot_general(a, b, (((1,), (1,)), ((), ())), preferred_element_type=HI)


def dot_nn(a, b):
    return lax.dot_general(a, b, (((1,), (0,)), ((), ())), preferred_element_type=HI)


def twice(a):
    return jnp.concatenate([a, a], axis=1)


def with_ones(values):
    return jnp.concatenate([values, jnp.ones_like(values)], axis=1)


def absorb(scores, values, state_max, state_out):
    width = scores.shape[1]
    new_max = jnp.maximum(state_max, jnp.max(scores, axis=1, keepdims=True))
    weights = jnp.exp2(scores - jnp.concatenate([new_max] * (width // DH), axis=1))
    mixed = dot_nn(weights.astype(LO), with_ones(values))
    if state_out is not None:
        mixed = state_out * twice(jnp.exp2(state_max - new_max)) + mixed
    return new_max, mixed


def on_diagonal():
    row = lax.broadcasted_iota(jnp.int32, (PIECE, DH), 0)
    return row == lax.broadcasted_iota(jnp.int32, (PIECE, DH), 1)


def encode_logsum(logsum):
    flat = jnp.sum(jnp.where(on_diagonal(), logsum, 0.0), axis=0, keepdims=True)
    flat = jnp.broadcast_to(flat, (EXTRA, DH))
    high = flat.astype(LO).astype(HI)
    middle = (flat - high).astype(LO).astype(HI)
    low = flat - high - middle
    row = lax.broadcasted_iota(jnp.int32, (EXTRA, DH), 0)
    return jnp.where(
        row == 0, high, jnp.where(row == 1, middle, jnp.where(row == 2, low, 0.0))
    ).astype(LO)


def decode_logsum(coded):
    parts = coded.astype(HI)
    flat = parts[0:1] + parts[1:2] + parts[2:3]
    own = jnp.where(on_diagonal(), jnp.broadcast_to(flat, (PIECE, DH)), 0.0)
    return jnp.broadcast_to(jnp.sum(own, axis=1, keepdims=True), (PIECE, DH))


def merge(pieces):
    logsums = [decode_logsum(p[PIECE:]) for p in pieces]
    top = logsums[0]
    for logsum in logsums[1:]:
        top = jnp.maximum(top, logsum)
    shares = [jnp.exp2(logsum - top) for logsum in logsums]
    total = sum(shares[1:], shares[0])
    mixed = None
    for share, piece in zip(shares, pieces):
        term = share * piece[:PIECE].astype(HI)
        mixed = term if mixed is None else mixed + term
    return mixed / total, top + jnp.log(total) * LOG2E


def kernel(
    lengths_ref, prompt_ref, asked_ref, new_ref, resident_ref, out_ref,
    cached, asked, spread, query_ref, wide, resident, fresh, state_max, state_out,
    part, swapped, joined, crossed,
    local_sems, resident_sems, near_send, near_recv, far_send, far_recv,
    relay_send, relay_recv, swap_send, swap_recv,
    cross_send, cross_recv, gather_send, gather_recv, forward_send, forward_recv,
    last_send, last_recv,
):
    samples = lengths_ref.shape[0]
    rows = query_ref.shape[0]
    core_rows = rows // 2
    blocks = core_rows // ROW_TILE
    step_rows = rows // STEPS
    heads = step_rows // samples
    slots = resident_ref.shape[2]
    tokens = prompt_ref.shape[1]
    group = lax.axis_index("group")
    seq = lax.axis_index("seq")
    x, core = seq // 2, lax.rem(seq, 2)
    core_start = core * core_rows
    other_group = {"group": 1 - group}
    other_core = {"seq": 2 * x + 1 - core}
    peers = [lax.rem(x + d, 4) for d in (1, 2, 3)]
    sources = [lax.rem(x + 4 - d, 4) for d in (1, 2, 3)]

    barrier = pltpu.get_barrier_semaphore()
    greeted = [other_group, other_core] + [
        {"seq": 2 * p + side} for p in peers for side in (0, 1)
    ]
    for device in greeted:
        pl.semaphore_signal(barrier, inc=1, device_id=device, device_id_type=MESH)

    prompt_copy = pltpu.make_async_copy(
        prompt_ref, cached.at[:, pl.ds(0, tokens)], local_sems.at[0]
    )
    prompt_copy.start()
    asked_copy = pltpu.make_async_copy(asked_ref, asked, local_sems.at[3])
    asked_copy.start()
    fresh_copies = [
        pltpu.make_async_copy(
            new_ref.at[kind, :, pl.ds(pl.multiple_of(seq * 16, 16), 16)],
            fresh.at[kind],
            local_sems.at[1 + kind],
        )
        for kind in (0, 1)
    ]
    for copy in fresh_copies:
        copy.start()
    chunks = resident_sems.shape[0]
    chunk = samples // chunks

    def resident_copy(index):
        return pltpu.make_async_copy(
            resident_ref.at[:, pl.ds(index * chunk, chunk)],
            resident.at[:, pl.ds(index * chunk, chunk)],
            resident_sems.at[index],
        )

    for index in range(chunks):
        resident_copy(index).start()

    def clear(index, carry):
        at = pl.ds(pl.multiple_of(index * 512, 512), 512)
        state_max[at] = jnp.full((512, DH), MASKED_SCORE, HI)
        state_out[at] = jnp.zeros((512, 2 * DH), HI)
        return carry

    lax.fori_loop(0, rows // 512, clear, 0)

    pl.semaphore_wait(barrier, len(greeted))
    def token_copies(source, source_start, start, send, recv, device):
        return [
            pltpu.make_async_remote_copy(
                src_ref=source.at[kind, pl.ds(source_start, tokens)],
                dst_ref=cached.at[kind, pl.ds(start, tokens)],
                send_sem=send.at[kind],
                recv_sem=recv.at[kind],
                device_id=device,
                device_id_type=MESH,
            )
            for kind in (0, 1)
        ]

    far_copies = token_copies(prompt_ref, 0, 2 * tokens, far_send, far_recv, other_group)
    near_copies = token_copies(prompt_ref, 0, tokens, near_send, near_recv, other_core)
    relay_copies = token_copies(
        cached, 2 * tokens, 3 * tokens, relay_send, relay_recv, other_core
    )
    for copy in far_copies + near_copies:
        copy.start()

    asked_copy.wait()

    def widen(index, carry):
        step, first = index // (samples // 16), 16 * lax.rem(index, samples // 16)
        base = pl.multiple_of(index * 16 * heads, 16 * heads)
        for head in range(heads):
            block = asked[step, pl.ds(pl.multiple_of(first, 16), 16), head * DH : (head + 1) * DH]
            spread[pl.ds(base + head, 16, stride=heads)] = block.astype(HI)
        at = pl.ds(base, 16 * heads)
        plain = spread[at]
        query_ref[at] = plain.astype(LO)
        scaled = plain * SCALE
        high = scaled.astype(LO)
        wide[at] = jnp.concatenate([high, (scaled - high.astype(HI)).astype(LO)], axis=1)
        return carry

    lax.fori_loop(0, STEPS * samples // 16, widen, 0)

    def gather_rows(ref, start, count):
        return jnp.concatenate(
            [ref[pl.ds(start + s * step_rows, count)] for s in range(STEPS)], axis=0
        )

    def scatter_rows(ref, start, count, value):
        for s in range(STEPS):
            ref[pl.ds(start + s * step_rows, count)] = value[s * count : (s + 1) * count]

    for copy in fresh_copies:
        copy.wait()
    new_rows = 16 * heads
    start = pl.multiple_of(seq * new_rows, new_rows)
    padding = jnp.zeros((DH - STEPS * 16, DH), LO)
    new_keys = jnp.concatenate([fresh[0, t] for t in range(STEPS)] + [padding], axis=0)
    new_values = jnp.concatenate([fresh[1, t] for t in range(STEPS)] + [padding], axis=0)
    scores = dot_nt(gather_rows(query_ref, start, new_rows), new_keys) * SCALE
    row = lax.broadcasted_iota(jnp.int32, scores.shape, 0)
    column = lax.broadcasted_iota(jnp.int32, scores.shape, 1)
    row_sample = lax.rem(row, new_rows) // heads
    seen = (column // 16 <= row // new_rows) & (lax.rem(column, 16) == row_sample)
    scores = jnp.where(seen, scores, MASKED_SCORE)
    top, mixed = absorb(
        scores, new_values, gather_rows(state_max, start, new_rows),
        gather_rows(state_out, start, new_rows),
    )
    scatter_rows(state_max, start, new_rows, top)
    scatter_rows(state_out, start, new_rows, mixed)

    pair_rows = 2 * heads
    shape = (STEPS * pair_rows, 2 * slots)
    column = lax.broadcasted_iota(jnp.int32, shape, 1)
    is_first = lax.rem(lax.broadcasted_iota(jnp.int32, shape, 0), pair_rows) < heads
    begin = jnp.where(is_first, 0, slots)

    def pair_scores(index):
        first = 2 * index
        start = pl.multiple_of(index * pair_rows, pair_rows)
        keys = resident[0, pl.ds(first, 2)].reshape(2 * slots, DH)
        scores = dot_nt(gather_rows(query_ref, start, pair_rows), keys) * SCALE
        here = seq * slots
        one = jnp.minimum(lengths_ref[first] - here, slots)
        two = jnp.minimum(lengths_ref[first + 1] - here, slots) + slots
        seen = (column >= begin) & (column < jnp.where(is_first, one, two))
        return jnp.where(seen, scores, MASKED_SCORE)

    def pair_weights(index, scores):
        start = pl.multiple_of(index * pair_rows, pair_rows)
        old = gather_rows(state_max, start, pair_rows)
        top = jnp.maximum(old, jnp.max(scores, axis=1, keepdims=True))
        return top, jnp.exp2(scores - twice(top)).astype(LO), jnp.exp2(old - top)

    def pair_mix(index, weights, decay):
        start = pl.multiple_of(index * pair_rows, pair_rows)
        values = resident[1, pl.ds(2 * index, 2)].reshape(2 * slots, DH)
        mixed = dot_nn(weights, with_ones(values))
        return gather_rows(state_out, start, pair_rows) * twice(decay) + mixed

    pairs = chunk // 2

    def resident_step(step, carry):
        resident_copy(step).wait()
        indices = [step * pairs + u for u in range(pairs)]
        scores = [pair_scores(index) for index in indices]
        weighed = [pair_weights(index, s) for index, s in zip(indices, scores)]
        mixes = [pair_mix(index, w[1], w[2]) for index, w in zip(indices, weighed)]
        for index, (top, _, _), mixed in zip(indices, weighed, mixes):
            start = pl.multiple_of(index * pair_rows, pair_rows)
            scatter_rows(state_max, start, pair_rows, top)
            scatter_rows(state_out, start, pair_rows, mixed)
        return carry

    lax.fori_loop(0, chunks, resident_step, 0)

    def piece_state(at):
        total = state_out[at, DH:]
        return state_out[at, :DH] / total, state_max[at] + jnp.log(total) * LOG2E

    def pack_step(index, carry):
        for u in range(4):
            start = (core_rows - core_start) + (4 * index + u) * PIECE
            mean, logsum = piece_state(pl.ds(pl.multiple_of(start, PIECE), PIECE))
            part[4 * index + u, 0:PIECE] = mean.astype(LO)
            part[4 * index + u, PIECE:] = encode_logsum(logsum)
        return carry

    lax.fori_loop(0, blocks, pack_step, 0)
    swap_copy = pltpu.make_async_remote_copy(
        src_ref=part, dst_ref=swapped, send_sem=swap_send, recv_sem=swap_recv,
        device_id=other_core, device_id_type=MESH,
    )
    swap_copy.start()

    def prompt_rows(begin, count, first, length):
        groups = [
            pl.ds(pl.multiple_of(begin + offset, GROUP_ROWS), GROUP_ROWS)
            for offset in range(0, count, GROUP_ROWS)
        ]
        state = [(state_max[at], state_out[at]) for at in groups]
        spans = [pl.ds(t, TOKEN_BLOCK) for t in range(first, first + length, TOKEN_BLOCK)]
        order = [(span, g) for span in spans for g in range(len(groups))]

        def scores_of(span, g):
            return dot_nt(wide[groups[g]], twice(cached[0, span]))

        following = scores_of(*order[0])
        for turn_index, (span, g) in enumerate(order):
            scores = following
            if turn_index + 1 < len(order):
                following = scores_of(*order[turn_index + 1])
            state[g] = absorb(scores, cached[1, span], *state[g])
        for at, (top, mixed) in zip(groups, state):
            state_max[at], state_out[at] = top, mixed

    def own_step(index, carry):
        prompt_rows(core_start + index * OWN_ROWS, OWN_ROWS, 0, 2 * tokens)
        return carry

    prompt_copy.wait()
    for copy in near_copies:
        copy.wait_recv()
    lax.fori_loop(0, core_rows // OWN_ROWS, own_step, 0)
    swap_copy.wait_recv()
    for far_copy, relay_copy in zip(far_copies, relay_copies):
        far_copy.wait_recv()
        relay_copy.start()

    def early_step(b, carry):
        prompt_rows(core_start + b * ROW_TILE, ROW_TILE, 2 * tokens, tokens)
        return carry

    lax.fori_loop(0, EARLY, early_step, 0)
    for relay_copy in relay_copies:
        relay_copy.wait_recv()

    def cross_copy(b, d):
        return pltpu.make_async_remote_copy(
            src_ref=joined.at[b, peers[d]], dst_ref=crossed.at[b, d],
            send_sem=cross_send.at[b, d], recv_sem=cross_recv.at[b, d],
            device_id={"seq": 2 * peers[d] + core}, device_id_type=MESH,
        )

    def piece_rows(b, owner):
        start = core_start + b * ROW_TILE + owner * PIECE
        return pl.ds(pl.multiple_of(start, PIECE), PIECE)

    def gather_copy(b, d, owner):
        at = piece_rows(b, owner)
        return pltpu.make_async_remote_copy(
            src_ref=out_ref.at[at], dst_ref=out_ref.at[at],
            send_sem=gather_send.at[b, d], recv_sem=gather_recv.at[b, d],
            device_id={"seq": 2 * peers[d] + core}, device_id_type=MESH,
        )

    def last_copy(d, owner):
        at = piece_rows(blocks - 1, owner)
        target = 2 * (x if d == 3 else peers[d]) + 1 - core
        return pltpu.make_async_remote_copy(
            src_ref=out_ref.at[at], dst_ref=out_ref.at[at],
            send_sem=last_send.at[d], recv_sem=last_recv.at[d],
            device_id={"seq": target}, device_id_type=MESH,
        )

    def forward_copy(b, side):
        start = side * core_rows + b * ROW_TILE
        at = pl.ds(pl.multiple_of(start, ROW_TILE), ROW_TILE)
        return pltpu.make_async_remote_copy(
            src_ref=out_ref.at[at], dst_ref=out_ref.at[at],
            send_sem=forward_send.at[b], recv_sem=forward_recv.at[b],
            device_id=other_core, device_id_type=MESH,
        )

    def far_tile(b):
        begin = core_start + b * ROW_TILE

        @pl.when(b < EARLY)
        def _():
            prompt_rows(begin, ROW_TILE, 3 * tokens, tokens)

        @pl.when(b >= EARLY)
        def _():
            prompt_rows(begin, ROW_TILE, 2 * tokens, 2 * tokens)

        for owner in range(4):
            at = piece_rows(b, owner)
            other = swapped[4 * b + owner]
            other_logsum = decode_logsum(other[PIECE:])
            top = jnp.maximum(state_max[at], other_logsum)
            decay, share = jnp.exp2(state_max[at] - top), jnp.exp2(other_logsum - top)
            total = state_out[at, DH:] * decay + share
            mixed = state_out[at, :DH] * decay + other[:PIECE].astype(HI) * share
            joined[b, owner, 0:PIECE] = (mixed / total).astype(LO)
            joined[b, owner, PIECE:] = encode_logsum(top + jnp.log(total) * LOG2E)
        for d in FARTHEST_FIRST:
            cross_copy(b, d).start()

    def join_chips(b):
        for d in range(3):
            cross_copy(b, d).wait_recv()
        mean, _ = merge([joined[b, x]] + [crossed[b, d] for d in range(3)])
        out_ref[piece_rows(b, x)] = mean.astype(LO)
        for d in FARTHEST_FIRST:
            gather_copy(b, d, x).start()

        @pl.when(b == blocks - 1)
        def _():
            for d in range(4):
                last_copy(d, x).start()

    def forward(b):
        for d in range(3):
            gather_copy(b, d, sources[d]).wait_recv()
        pl.when(b < blocks - 1)(lambda: forward_copy(b, core).start())

    def turn(b, carry):
        pl.when(b < blocks)(lambda: far_tile(b))
        late, last = (b - lag for lag in LAGS)
        pl.when((late >= 0) & (late < blocks))(lambda: join_chips(late))
        pl.when(last >= 0)(lambda: forward(last))
        return carry

    lax.fori_loop(0, blocks + LAGS[1], turn, 0)

    for copy in far_copies + near_copies + relay_copies + [swap_copy]:
        copy.wait_send()

    def finish(b, carry):
        for d in range(3):
            cross_copy(b, d).wait_send()
            gather_copy(b, d, x).wait_send()

        @pl.when(b < blocks - 1)
        def _():
            forward_copy(b, core).wait_send()
            forward_copy(b, 1 - core).wait_recv()

        return carry

    lax.fori_loop(0, blocks, finish, 0)
    for d in range(4):
        last_copy(d, x).wait_send()
        at = pl.ds(
            pl.multiple_of(core_rows - core_start + (blocks - 1) * ROW_TILE, PIECE), ROW_TILE
        )
        owner = x if d == 3 else sources[d]
        piece = out_ref.at[at].at[pl.ds(pl.multiple_of(owner * PIECE, PIECE), PIECE)]
        pltpu.make_async_remote_copy(
            src_ref=piece, dst_ref=piece, send_sem=last_send.at[d], recv_sem=last_recv.at[d],
            device_id=other_core, device_id_type=MESH,
        ).wait_recv()


def local(prompt_kv, queries, new_kv, resident_kv, seq_lengths):
    steps, samples, columns = queries.shape
    heads = columns // DH
    rows = steps * samples * heads
    blocks = rows // 2 // ROW_TILE
    piece = (PIECE + EXTRA, DH)
    dma = pltpu.SemaphoreType.DMA
    anywhere = pl.BlockSpec(memory_space=pl.ANY)
    in_vmem = pl.BlockSpec(memory_space=pltpu.VMEM)
    out = pl.pallas_call(
        kernel,
        out_shape=jax.ShapeDtypeStruct((rows, DH), LO),
        in_specs=[pl.BlockSpec(memory_space=pltpu.SMEM), anywhere, anywhere, anywhere, anywhere],
        out_specs=in_vmem,
        scratch_shapes=[
            pltpu.VMEM((2, 4 * prompt_kv.shape[1], DH), LO),
            pltpu.VMEM(queries.shape, LO),
            pltpu.VMEM((rows, DH), HI),
            pltpu.VMEM((rows, DH), LO),
            pltpu.VMEM((rows, 2 * DH), LO),
            pltpu.VMEM(resident_kv.shape, LO),
            pltpu.VMEM((2, steps, 16, DH), LO),
            pltpu.VMEM((rows, DH), HI),
            pltpu.VMEM((rows, 2 * DH), HI),
            pltpu.VMEM((4 * blocks,) + piece, LO),
            pltpu.VMEM((4 * blocks,) + piece, LO),
            pltpu.VMEM((blocks, 4) + piece, LO),
            pltpu.VMEM((blocks, 3) + piece, LO),
            dma((4,)), dma((4,)), dma((2,)), dma((2,)), dma((2,)), dma((2,)),
            dma((2,)), dma((2,)), dma, dma,
            dma((blocks, 3)), dma((blocks, 3)), dma((blocks, 3)), dma((blocks, 3)),
            dma((blocks,)), dma((blocks,)), dma((4,)), dma((4,)),
        ],
        compiler_params=pltpu.CompilerParams(
            collective_id=0, has_side_effects=True, vmem_limit_bytes=48 * 2**20
        ),
    )(seq_lengths, prompt_kv, queries, new_kv, resident_kv)
    return out.reshape(queries.shape)


def solution(mesh):
    placed = (
        P(None, ("group", "seq"), "head"),
        P(None, "group", "head"),
        P(None, None, "group", "head"),
        P(None, "group", "seq", "head"),
        P("group"),
    )
    return jax.shard_map(
        local, mesh=mesh, in_specs=placed, out_specs=P(None, "group", "head"), check_vma=False
    )
```
